32 devices in a mesh: seq: 8 (over z, core), kvh: 4 (over y, x).
Axes of the slice: x: 2, y: 2, z: 4, core: 2. Of those that a mesh axis runs over, the one named last changes fastest.
Arguments:
- normed: bfloat16 [2048, 4096], P('seq'), may hold values from -8 to 8
- w_query: bfloat16 [4096, 4096], P(None, 'kvh'), may hold values from -1 to 1, as said below
- w_key: bfloat16 [4096, 1024], P(None, 'kvh'), may hold values from -1 to 1, as said below
- w_value: bfloat16 [4096, 1024], P(None, 'kvh'), may hold values from -0.09375 to 0.09375
- positions: int32 [2048], P('seq'), may hold values from 0 to 2174, as said below
- block_mask: int32 [16, 16], P('seq'), may hold values from 0 to 1, as said below
- grad_attn: bfloat16 [2048, 4096], P('seq', 'kvh'), may hold values from -6 to 6
Outputs:
- grad_normed: bfloat16 [2048, 4096], P('seq', 'kvh')
- grad_wq: float32 [4096, 4096], P('seq', 'kvh')
- grad_wk: float32 [4096, 1024], P('seq', 'kvh')
- grad_wv: float32 [4096, 1024], P('seq', 'kvh')
The draws below stay inside these ranges and needn't reach their ends.
Inputs may be any that keep to these rules, and one draw needn't show every extreme that they name: Within a block positions rise by one per token; block b starts between b * 128 and (b + 1) * 128 - 1, block 0 at 0, the last block at its latest start. `block_mask`: the diagonal is 1; a block may read only blocks of earlier rounds besides itself; entries for earlier rounds are 0 or 1. `w_query`: entries of about 4096^(-1/2) in size. `w_key`: entries of about 4096^(-1/2) in size.
All inputs are finite; a program needn't handle non-finite values.
Results may differ from the reference program's by a relative error of at most 0.019.
The reference program's roundings to bfloat16 on the way (of `values`, `weights` and `grad_scores`) count: a program that leaves them out, or rounds other values in their place, can miss the bound.
Values may be sent and summed in bfloat16 or wider, within the bound.
A program may use at most 128 MiB of HBM per device.

```python
import jax
import jax.numpy as jnp
from jax import lax

D = 4096
HEADS = 32
KV_HEADS = 8
HEAD = 128
GROUP = 4
BLOCK = 128
AGENTS = 4
BLOCKS = 16
TOKENS = 2048


def draw_positions(key, part):
    offsets = jax.random.randint(key, (BLOCKS,), 0, BLOCK)
    block_index = jnp.arange(BLOCKS)
    offsets = jnp.where(block_index == 0, 0, offsets)
    offsets = jnp.where(block_index == BLOCKS - 1, BLOCK - 1, offsets)
    starts = block_index * BLOCK + offsets
    return (starts[:, None] + jnp.arange(BLOCK)[None, :]).reshape(BLOCKS * BLOCK).astype(jnp.int32)


def draw_block_mask(key, part):
    block_index = jnp.arange(BLOCKS)
    round_index = block_index // AGENTS
    coins = jax.random.randint(key, (BLOCKS, BLOCKS), 0, 4)
    earlier = round_index[None, :] < round_index[:, None]
    diagonal = block_index[:, None] == block_index[None, :]
    return jnp.where(diagonal, 1, jnp.where(earlier & (coins > 0), 1, 0)).astype(jnp.int32)


def projection_pair(key):
    seed_query = jax.random.fold_in(key, 101)
    seed_keys = jax.random.fold_in(key, 102)
    spread = D ** (-0.5)
    query_weight = jnp.clip(jax.random.normal(seed_query, (D, HEADS * HEAD), jnp.float32), -6.0, 6.0) * spread
    key_weight = jnp.clip(jax.random.normal(seed_keys, (D, KV_HEADS * HEAD), jnp.float32), -6.0, 6.0) * spread
    return (query_weight, key_weight)


def draw_w_query(key, part):
    return projection_pair(key)[0].astype(jnp.bfloat16)


def draw_w_key(key, part):
    return projection_pair(key)[1].astype(jnp.bfloat16)


def draw_normed(key, part):
    return jnp.clip(jax.random.normal(jax.random.fold_in(key, 103), (TOKENS, D), jnp.float32), -6.0, 6.0).astype(jnp.bfloat16)


def block_scale(own_key, extent, cuts, low, top_value):
    factor_of, own = 1.0, jax.random.fold_in(own_key, 6)
    for axis_at, blocks in cuts:
        heights = jnp.exp(jax.random.uniform(jax.random.fold_in(own, axis_at), (blocks,), jnp.float32, low / len(cuts), top_value / len(cuts)))
        factor_of = factor_of * jnp.repeat(heights, extent[axis_at] // blocks).reshape([-1 if axis == axis_at else 1 for axis in range(len(extent))])
    return factor_of


def centred(own_key, shape, width, most, cuts=(), held_as=jnp.bfloat16):
    gain = block_scale(own_key, shape, cuts, -0.22, 0.18) if cuts else 1.0
    result = jax.random.normal(own_key, shape, jnp.float32) * width * gain
    return jnp.minimum(jnp.maximum(result, -most), most).astype(held_as)


def setup_inputs(seed: int = 0) -> dict:
    arg_keys = jax.random.split(jax.random.key(seed), 8)
    return {
        "normed": draw_normed(jax.random.fold_in(arg_keys[7], 71), 0),
        "w_query": draw_w_query(jax.random.fold_in(arg_keys[7], 71), 0),
        "w_key": draw_w_key(jax.random.fold_in(arg_keys[7], 71), 0),
        "w_value": centred(arg_keys[3], (D, KV_HEADS * HEAD), D ** -0.5, 0.09375, ((1, 4),)),
        "positions": draw_positions(jax.random.fold_in(arg_keys[7], 71), 0),
        "block_mask": draw_block_mask(jax.random.fold_in(arg_keys[7], 71), 0),
        "grad_attn": centred(arg_keys[6], (TOKENS, HEADS * HEAD), 1.0, 6.0, ((0, 8), (1, 4))),
    }


THETA = 500000.0


def rotate(values, positions, rotation_sign):
    tok_rows = values.shape[0]
    head_count = values.shape[1] // HEAD
    half_size = HEAD // 2
    pieces = values.reshape(tok_rows, head_count, HEAD)
    frequency = THETA ** (-(jnp.arange(half_size, dtype=jnp.float32) * (2.0 / HEAD)))
    angles = positions.astype(jnp.float32)[:, None] * frequency[None, :]
    cosine = jnp.cos(angles)[:, None, :]
    sine_part = rotation_sign * jnp.sin(angles)[:, None, :]
    lower_half = pieces[:, :, :half_size]
    upper_half = pieces[:, :, half_size:]
    turned = jnp.concatenate([lower_half * cosine - upper_half * sine_part, upper_half * cosine + lower_half * sine_part], axis=2)
    return turned.reshape(tok_rows, head_count * HEAD)


def visible(mask_table, query_block0, query_count, key_block0, key_count):
    query_local = jnp.arange(query_count)
    key_local = jnp.arange(key_count)
    query_block = query_block0 + query_local // BLOCK
    key_block = key_block0 + key_local // BLOCK
    allowed = jnp.repeat(jnp.repeat(mask_table, BLOCK, axis=0), BLOCK, axis=1) == 1
    inner_ok = (key_local % BLOCK)[None, :] <= (query_local % BLOCK)[:, None]
    return allowed & ((query_block[:, None] != key_block[None, :]) | inner_ok)


def product(form, left, right):
    return jnp.einsum(form, left.astype(jnp.float32), right.astype(jnp.float32))


def head_group(queries, keys, values, grad_heads, seen):
    score_scale = HEAD ** -0.5
    scores = product('tgd,sd->gts', queries, keys) * score_scale
    scores = jnp.where(seen[None], scores, -1e30)
    row_max = jnp.max(scores, axis=2, keepdims=True)
    log_total = row_max[:, :, 0] + jnp.log(jnp.sum(jnp.exp(scores - row_max), axis=2))
    probs = jnp.where(seen[None], jnp.exp(scores - log_total[:, :, None]), 0.0)
    weights = probs.astype(jnp.bfloat16)
    outputs = product('gts,sd->gtd', weights, values)
    row_dots = jnp.sum(outputs * jnp.transpose(grad_heads.astype(jnp.float32), (1, 0, 2)), axis=2)
    grad_probs = product('tgd,sd->gts', grad_heads, values)
    grad_scores = (probs * (grad_probs - row_dots[:, :, None]) * score_scale).astype(jnp.bfloat16)
    grad_query = product('gts,sd->tgd', grad_scores, keys)
    grad_key = product('gts,tgd->sd', grad_scores, queries)
    grad_value = product('gts,tgd->sd', weights, grad_heads)
    return grad_query, grad_key, grad_value


def reference(normed, w_query, w_key, w_value, positions, block_mask, grad_attn):
    tokens = normed.shape[0]
    queries = rotate(jnp.dot(normed, w_query, preferred_element_type=jnp.float32), positions, 1.0).astype(jnp.bfloat16)
    keys = rotate(jnp.dot(normed, w_key, preferred_element_type=jnp.float32), positions, 1.0).astype(jnp.bfloat16)
    values = jnp.dot(normed, w_value, preferred_element_type=jnp.float32).astype(jnp.bfloat16)
    seen = visible(block_mask, 0, tokens, 0, tokens)
    query_groups = jnp.transpose(queries.reshape(tokens, KV_HEADS, GROUP, HEAD), (1, 0, 2, 3))
    grad_groups = jnp.transpose(grad_attn.reshape(tokens, KV_HEADS, GROUP, HEAD), (1, 0, 2, 3))
    key_groups = jnp.transpose(keys.reshape(tokens, KV_HEADS, HEAD), (1, 0, 2))
    value_groups = jnp.transpose(values.reshape(tokens, KV_HEADS, HEAD), (1, 0, 2))
    grad_query, grad_key, grad_value = lax.map(lambda items: head_group(items[0], items[1], items[2], items[3], seen), (query_groups, key_groups, value_groups, grad_groups))
    grad_query = jnp.transpose(grad_query, (1, 0, 2, 3)).reshape(tokens, HEADS * HEAD)
    grad_key = jnp.transpose(grad_key, (1, 0, 2)).reshape(tokens, KV_HEADS * HEAD)
    grad_value = jnp.transpose(grad_value, (1, 0, 2)).reshape(tokens, KV_HEADS * HEAD)
    query_grad = rotate(grad_query, positions, -1.0).astype(jnp.bfloat16)
    key_grad = rotate(grad_key, positions, -1.0).astype(jnp.bfloat16)
    value_grad = grad_value.astype(jnp.bfloat16)
    grad_wq = jnp.dot(normed.T, query_grad, preferred_element_type=jnp.float32)
    grad_wk = jnp.dot(normed.T, key_grad, preferred_element_type=jnp.float32)
    grad_wv = jnp.dot(normed.T, value_grad, preferred_element_type=jnp.float32)
    grad_normed = jnp.dot(query_grad, w_query.T, preferred_element_type=jnp.float32)
    grad_normed = grad_normed + jnp.dot(key_grad, w_key.T, preferred_element_type=jnp.float32)
    grad_normed = grad_normed + jnp.dot(value_grad, w_value.T, preferred_element_type=jnp.float32)
    return (grad_normed.astype(jnp.bfloat16), grad_wq, grad_wk, grad_wv)
```

```python
import functools
import math

import jax
import jax.numpy as jnp
from jax import lax
from jax.experimental import pallas as pl
from jax.experimental.pallas import tpu as pltpu
from jax.sharding import PartitionSpec as P

HEAD = 128
HALF = 64
BLOCK = 128
THETA = 500000.0
SCALE = HEAD**-0.5
LOG2E = math.log2(math.e)
MESH = pl.DeviceIdType.MESH
ANY = pl.BlockSpec(memory_space=pl.ANY)
VMEM = pl.BlockSpec(memory_space=pltpu.VMEM)


def params(collective=None, semantics=None):
    extra = {}
    if collective is not None:
        extra = dict(collective_id=collective, has_side_effects=True)
    if semantics is not None:
        extra["dimension_semantics"] = semantics
    return pltpu.CompilerParams(vmem_limit_bytes=56 * 1024 * 1024, **extra)


def gather_kernel(chips, own, out, local_sem, send_r, send_l, send_p, recv_l, recv_r, recv_p):
    me = lax.axis_index("seq")
    chip, core = me // 2, me % 2
    has_left, has_right = chip > 0, chip < chips - 1
    mine = pltpu.make_async_copy(own, out.at[me], local_sem)
    mine.start()
    barrier = pltpu.get_barrier_semaphore()

    def greet(device):
        pl.semaphore_signal(barrier, inc=1, device_id={"seq": device}, device_id_type=MESH)

    greet(chip * 2 + 1 - core)
    pl.when(has_left)(lambda: greet(me - 2))
    pl.when(has_right)(lambda: greet(me + 2))
    pl.semaphore_wait(barrier, 1 + has_left.astype(jnp.int32) + has_right.astype(jnp.int32))

    def remote(src, slot, send, recv, device):
        return pltpu.make_async_remote_copy(
            src_ref=src,
            dst_ref=out.at[slot],
            send_sem=send,
            recv_sem=recv,
            device_id={"seq": device},
            device_id_type=MESH,
        )

    def source(distance, slot):
        return own if distance == 0 else out.at[slot]

    def right(t):
        slot = me - 2 * t
        return remote(source(t, slot), slot, send_r.at[t], recv_l.at[t + 1], me + 2)

    def left(t):
        slot = me + 2 * t
        return remote(source(t, slot), slot, send_l.at[t], recv_r.at[t + 1], me - 2)

    def partner(offset):
        slot = me + 2 * offset
        at = offset + chips - 1
        return remote(
            source(abs(offset), slot), slot, send_p.at[at], recv_p.at[at], chip * 2 + 1 - core
        )

    def arrival(slot, sem):
        pltpu.make_async_copy(out.at[slot], out.at[slot], sem).wait()

    pl.when(has_right)(lambda: right(0).start())
    pl.when(has_left)(lambda: left(0).start())
    partner(0).start()
    for t in range(1, chips):

        @pl.when(chip - t >= 0)
        def _():
            arrival(me - 2 * t, recv_l.at[t])
            if t < chips - 1:
                pl.when(has_right)(lambda: right(t).start())
            partner(-t).start()

        @pl.when(chip + t < chips)
        def _():
            arrival(me + 2 * t, recv_r.at[t])
            if t < chips - 1:
                pl.when(has_left)(lambda: left(t).start())
            partner(t).start()

    mine.wait()
    other = chip * 2 + 1 - core
    for t in range(chips):

        @pl.when(chip - t >= 0)
        def _():
            arrival(other - 2 * t, recv_p.at[chips - 1 - t])
            partner(-t).wait_send()
            if t < chips - 1:
                pl.when(has_right)(lambda: right(t).wait_send())

        @pl.when(chip + t < chips)
        def _():
            if t > 0:
                arrival(other + 2 * t, recv_p.at[chips - 1 + t])
                partner(t).wait_send()
            if t < chips - 1:
                pl.when(has_left)(lambda: left(t).wait_send())


def gather(block, devices, collective):
    chips = devices // 2
    dma = pltpu.SemaphoreType.DMA
    out = pl.pallas_call(
        functools.partial(gather_kernel, chips),
        out_shape=jax.ShapeDtypeStruct((devices,) + block.shape, block.dtype),
        in_specs=[ANY],
        out_specs=ANY,
        scratch_shapes=[
            dma(()),
            dma((chips,)),
            dma((chips,)),
            dma((2 * chips,)),
            dma((chips + 1,)),
            dma((chips + 1,)),
            dma((2 * chips,)),
        ],
        compiler_params=params(collective),
        cost_estimate=pl.CostEstimate(
            flops=0, bytes_accessed=24 * devices * block.size, transcendentals=0
        ),
    )(block)
    return out.reshape(devices * block.shape[0], block.shape[1])


def reduce_kernel(
    chips, part, out, from_partner, summed, arrived, send_p, recv_p, send_z, recv_z
):
    me = lax.axis_index("seq")
    chip, core = me // 2, me % 2
    other = chip * 2 + 1 - core
    barrier = pltpu.get_barrier_semaphore()

    def greet(device):
        pl.semaphore_signal(barrier, inc=1, device_id={"seq": device}, device_id_type=MESH)

    greet(other)
    for t in range(1, chips):
        greet(((chip + t) % chips) * 2 + core)
    pl.semaphore_wait(barrier, chips)

    def to_partner(t):
        return pltpu.make_async_remote_copy(
            src_ref=part.at[((chip + t) % chips) * 2 + 1 - core],
            dst_ref=from_partner.at[t],
            send_sem=send_p.at[t],
            recv_sem=recv_p.at[t],
            device_id={"seq": other},
            device_id_type=MESH,
        )

    def to_owner(t):
        return pltpu.make_async_remote_copy(
            src_ref=summed.at[t],
            dst_ref=arrived.at[t],
            send_sem=send_z.at[t],
            recv_sem=recv_z.at[t],
            device_id={"seq": ((chip + t) % chips) * 2 + core},
            device_id_type=MESH,
        )

    order = list(range(1, chips)) + [0]
    for t in order:
        to_partner(t).start()
    for t in order:
        to_partner(t).wait()
        total = part[((chip + t) % chips) * 2 + core].astype(jnp.float32) + from_partner[t].astype(
            jnp.float32
        )
        if t:
            summed[t] = total.astype(summed.dtype)
            to_owner(t).start()
        else:
            out[...] = total
    for t in range(1, chips):
        to_owner(t).wait()
        out[...] += arrived[t].astype(jnp.float32)


def reduce_to_owner(part, devices, collective):
    chips = devices // 2
    rows, cols = part.shape[0] // devices, part.shape[1]
    dma = pltpu.SemaphoreType.DMA((chips,))
    slots = pltpu.VMEM((chips, rows, cols), part.dtype)
    return pl.pallas_call(
        functools.partial(reduce_kernel, chips),
        out_shape=jax.ShapeDtypeStruct((rows, cols), jnp.float32),
        in_specs=[VMEM],
        out_specs=VMEM,
        scratch_shapes=[slots, slots, slots, dma, dma, dma, dma],
        compiler_params=params(collective),
        cost_estimate=pl.CostEstimate(
            flops=0, bytes_accessed=24 * part.size, transcendentals=0
        ),
    )(part.reshape(devices, rows, cols))


def dot(left, right, contract):
    return lax.dot_general(
        left, right, ((contract[:1], contract[1:]), ((), ())), preferred_element_type=jnp.float32
    )


def attention_kernel(
    group, chunk, mask, first, q, g, k, v, cos_t, sin_t, dq, dk, dv, bias, scores, gprobs, weights,
    k_t, dk_sum, dv_sum
):
    step = pl.program_id(0)
    keys, tokens = bias.shape
    chunks = [pl.ds(c * chunk, chunk) for c in range(keys // chunk)]

    @pl.when(step == 0)
    def _():
        key_at = lax.broadcasted_iota(jnp.int32, (BLOCK, BLOCK), 0)
        query_at = lax.broadcasted_iota(jnp.int32, (BLOCK, BLOCK), 1)
        lower = jnp.where(key_at <= query_at, 0.0, -1e30).astype(jnp.float32)
        for i in range(tokens // BLOCK):
            def fill(j, _, i=i):
                shown = jnp.where(mask[i, j] == 1, 0.0, -1e30).astype(jnp.float32)
                inner = jnp.where(j == first[0] + i, 1.0, 0.0).astype(jnp.float32)
                rows = pl.ds(pl.multiple_of(j * BLOCK, BLOCK), BLOCK)
                bias[rows, i * BLOCK : (i + 1) * BLOCK] = lower * inner + shown
                return 0

            lax.fori_loop(0, keys // BLOCK, fill, 0)

    @pl.when(step % group == 0)
    def _():
        k_t[...] = k[...].T
        dk_sum[...] = jnp.zeros_like(dk_sum)
        dv_sum[...] = jnp.zeros_like(dv_sum)

    qh, gh = q[...], g[...]
    top = jnp.full((1, tokens), -3e38, jnp.float32)
    for at in chunks:
        s = dot(k[at, :], qh, (1, 1)) * (SCALE * LOG2E) + bias[at, :]
        scores[at, :] = s
        gprobs[at, :] = dot(v[at, :], gh, (1, 1))
        top = jnp.maximum(top, jnp.max(s, axis=0, keepdims=True))
    total = jnp.zeros((1, tokens), jnp.float32)
    for at in chunks:
        e = jnp.exp2(scores[at, :] - top)
        scores[at, :] = e
        total = total + jnp.sum(e, axis=0, keepdims=True)
    inverse = 1.0 / total
    row_dots = jnp.zeros((1, tokens), jnp.float32)
    for at in chunks:
        w = (scores[at, :] * inverse).astype(jnp.bfloat16)
        weights[at, :] = w
        row_dots = row_dots + jnp.sum(
            w.astype(jnp.float32) * gprobs[at, :], axis=0, keepdims=True
        )
    inverse_scaled = inverse * SCALE
    dq_t = jnp.zeros((HEAD, tokens), jnp.float32)
    for at in chunks:
        ds = ((scores[at, :] * inverse_scaled) * (gprobs[at, :] - row_dots)).astype(jnp.bfloat16)
        dk_sum[at, :] += dot(ds, qh, (1, 0))
        dv_sum[at, :] += dot(weights[at, :], gh, (1, 0))
        dq_t = dq_t + dot(k_t[:, at], ds, (1, 0))
    low, high = dq_t[:HALF, :], dq_t[HALF:, :]
    c, s = cos_t[...], sin_t[...]
    turned = jnp.concatenate([low * c + high * s, high * c - low * s], axis=0)
    dq[...] = turned.T.astype(jnp.bfloat16)

    @pl.when(step % group == group - 1)
    def _():
        dk[...] = dk_sum[...].astype(jnp.bfloat16)
        dv[...] = dv_sum[...].astype(jnp.bfloat16)


def attention(queries, grad_attn, keys_values, mask, first, cos_t, sin_t, kv_local):
    tokens = queries.shape[0]
    heads = queries.shape[1] // HEAD
    group = heads // kv_local
    keys = keys_values.shape[0]
    f32, bf16 = jnp.float32, jnp.bfloat16
    one_head = pl.BlockSpec((tokens, HEAD), lambda h: (0, h))
    angle = pl.BlockSpec((HALF, tokens), lambda h: (0, 0))
    smem = pl.BlockSpec(memory_space=pltpu.SMEM)
    return pl.pallas_call(
        functools.partial(attention_kernel, group, 512),
        grid=(heads,),
        out_shape=[
            jax.ShapeDtypeStruct((tokens, heads * HEAD), bf16),
            jax.ShapeDtypeStruct((keys, kv_local * HEAD), bf16),
            jax.ShapeDtypeStruct((keys, kv_local * HEAD), bf16),
        ],
        in_specs=[
            smem,
            smem,
            one_head,
            one_head,
            pl.BlockSpec((keys, HEAD), lambda h: (0, h // group)),
            pl.BlockSpec((keys, HEAD), lambda h: (0, kv_local + h // group)),
            angle,
            angle,
        ],
        out_specs=[
            one_head,
            pl.BlockSpec((keys, HEAD), lambda h: (0, h // group)),
            pl.BlockSpec((keys, HEAD), lambda h: (0, h // group)),
        ],
        scratch_shapes=[
            pltpu.VMEM((keys, tokens), f32),
            pltpu.VMEM((keys, tokens), f32),
            pltpu.VMEM((keys, tokens), f32),
            pltpu.VMEM((keys, tokens), bf16),
            pltpu.VMEM((HEAD, keys), bf16),
            pltpu.VMEM((keys, HEAD), f32),
            pltpu.VMEM((keys, HEAD), f32),
        ],
        compiler_params=params(None, ("arbitrary",)),
        cost_estimate=pl.CostEstimate(
            flops=10 * keys * tokens * heads * HEAD,
            bytes_accessed=8 * keys * HEAD * kv_local,
            transcendentals=heads * keys * tokens,
        ),
    )(mask, first, queries, grad_attn, keys_values, keys_values, cos_t, sin_t)


def rotate(values, cosine, sine):
    rows = values.shape[0]
    pieces = values.reshape(rows, -1, HEAD)
    low, high = pieces[:, :, :HALF], pieces[:, :, HALF:]
    c, s = cosine[:, None, :], sine[:, None, :]
    return jnp.concatenate([low * c - high * s, high * c + low * s], axis=2).reshape(rows, -1)


def body(devices, groups, normed, w_query, w_key, w_value, positions, block_mask, grad_attn):
    tokens, width = normed.shape
    kv_cols = w_key.shape[1]
    kv_local = kv_cols // HEAD
    q_cols = w_query.shape[1]
    me = lax.axis_index("seq")
    part = width // devices // groups
    my_part = lax.dynamic_slice_in_dim(
        normed.reshape(tokens, devices, groups * part), lax.axis_index("kvh") * part, part, 2
    )
    columns = lax.all_to_all(
        my_part.reshape(tokens, devices * part), "seq", split_axis=1, concat_axis=0, tiled=True
    )
    columns = lax.all_gather(columns, "kvh", axis=1, tiled=True)

    frequency = THETA ** (-(jnp.arange(HALF, dtype=jnp.float32) * (2.0 / HEAD)))
    angles = positions.astype(jnp.float32)[:, None] * frequency[None, :]
    cosine, sine = jnp.cos(angles), jnp.sin(angles)

    def project(weight):
        return jnp.dot(normed, weight, preferred_element_type=jnp.float32)

    keys = rotate(project(w_key), cosine, sine).astype(jnp.bfloat16)
    values = project(w_value).astype(jnp.bfloat16)
    queries = rotate(project(w_query), cosine, sine).astype(jnp.bfloat16)
    keys_values = gather(jnp.concatenate([keys, values], axis=1), devices, 1)
    first = (me * (tokens // BLOCK)).astype(jnp.int32).reshape(1)
    dq, dk_part, dv_part = attention(
        queries, grad_attn, keys_values, block_mask, first, cosine.T, sine.T, kv_local
    )
    kv_total = reduce_to_owner(jnp.concatenate([dk_part, dv_part], axis=1), devices, 2)
    dk = rotate(kv_total[:, :kv_cols], cosine, -sine).astype(jnp.bfloat16)
    dv = kv_total[:, kv_cols:].astype(jnp.bfloat16)

    partial = dot(dq, w_query, (1, 1)) + dot(dk, w_key, (1, 1)) + dot(dv, w_value, (1, 1))
    grad_normed = lax.psum_scatter(
        partial.astype(jnp.bfloat16), "kvh", scatter_dimension=1, tiled=True
    )
    joined = gather(jnp.concatenate([dq, dk, dv], axis=1), devices, 3)
    grad_wq = dot(columns, joined[:, :q_cols], (0, 0))
    grad_wk = dot(columns, joined[:, q_cols : q_cols + kv_cols], (0, 0))
    grad_wv = dot(columns, joined[:, q_cols + kv_cols :], (0, 0))
    return (grad_normed, grad_wq, grad_wk, grad_wv)


def solution(mesh):
    in_specs = (
        P("seq", None),
        P(None, "kvh"),
        P(None, "kvh"),
        P(None, "kvh"),
        P("seq"),
        P("seq", None),
        P("seq", "kvh"),
    )
    out_specs = (P("seq", "kvh"),) * 4
    return jax.shard_map(
        functools.partial(body, mesh.shape["seq"], mesh.shape["kvh"]),
        mesh=mesh,
        in_specs=in_specs,
        out_specs=out_specs,
        check_vma=False,
    )
```

```python
import functools
import math

import jax
import jax.numpy as jnp
from jax import lax
from jax.experimental import pallas as pl
from jax.experimental.pallas import tpu as pltpu
from jax.sharding import PartitionSpec as P

HEAD = 128
HALF = 64
BLOCK = 128
THETA = 500000.0
SCALE = HEAD**-0.5
LOG2E = math.log2(math.e)
MESH = pl.DeviceIdType.MESH
ANY = pl.BlockSpec(memory_space=pl.ANY)
VMEM = pl.BlockSpec(memory_space=pltpu.VMEM)


def params(collective=None, semantics=None):
    extra = {}
    if collective is not None:
        extra = dict(collective_id=collective, has_side_effects=True)
    if semantics is not None:
        extra["dimension_semantics"] = semantics
    return pltpu.CompilerParams(vmem_limit_bytes=56 * 1024 * 1024, **extra)


def gather_kernel(chips, own, out, local_sem, send_r, send_l, send_p, recv_l, recv_r, recv_p):
    me = lax.axis_index("seq")
    chip, core = me // 2, me % 2
    has_left, has_right = chip > 0, chip < chips - 1
    mine = pltpu.make_async_copy(own, out.at[me], local_sem)
    mine.start()
    barrier = pltpu.get_barrier_semaphore()

    def greet(device):
        pl.semaphore_signal(barrier, inc=1, device_id={"seq": device}, device_id_type=MESH)

    greet(chip * 2 + 1 - core)
    pl.when(has_left)(lambda: greet(me - 2))
    pl.when(has_right)(lambda: greet(me + 2))
    pl.semaphore_wait(barrier, 1 + has_left.astype(jnp.int32) + has_right.astype(jnp.int32))

    def remote(src, slot, send, recv, device):
        return pltpu.make_async_remote_copy(
            src_ref=src,
            dst_ref=out.at[slot],
            send_sem=send,
            recv_sem=recv,
            device_id={"seq": device},
            device_id_type=MESH,
        )

    def source(distance, slot):
        return own if distance == 0 else out.at[slot]

    def right(t):
        slot = me - 2 * t
        return remote(source(t, slot), slot, send_r.at[t], recv_l.at[t + 1], me + 2)

    def left(t):
        slot = me + 2 * t
        return remote(source(t, slot), slot, send_l.at[t], recv_r.at[t + 1], me - 2)

    def partner(offset):
        slot = me + 2 * offset
        at = offset + chips - 1
        return remote(
            source(abs(offset), slot), slot, send_p.at[at], recv_p.at[at], chip * 2 + 1 - core
        )

    def arrival(slot, sem):
        pltpu.make_async_copy(out.at[slot], out.at[slot], sem).wait()

    pl.when(has_right)(lambda: right(0).start())
    pl.when(has_left)(lambda: left(0).start())
    partner(0).start()
    for t in range(1, chips):

        @pl.when(chip - t >= 0)
        def _():
            arrival(me - 2 * t, recv_l.at[t])
            if t < chips - 1:
                pl.when(has_right)(lambda: right(t).start())
            partner(-t).start()

        @pl.when(chip + t < chips)
        def _():
            arrival(me + 2 * t, recv_r.at[t])
            if t < chips - 1:
                pl.when(has_left)(lambda: left(t).start())
            partner(t).start()

    mine.wait()
    other = chip * 2 + 1 - core
    for t in range(chips):

        @pl.when(chip - t >= 0)
        def _():
            arrival(other - 2 * t, recv_p.at[chips - 1 - t])
            partner(-t).wait_send()
            if t < chips - 1:
                pl.when(has_right)(lambda: right(t).wait_send())

        @pl.when(chip + t < chips)
        def _():
            if t > 0:
                arrival(other + 2 * t, recv_p.at[chips - 1 + t])
                partner(t).wait_send()
            if t < chips - 1:
                pl.when(has_left)(lambda: left(t).wait_send())


def gather(block, devices, collective):
    chips = devices // 2
    dma = pltpu.SemaphoreType.DMA
    out = pl.pallas_call(
        functools.partial(gather_kernel, chips),
        out_shape=jax.ShapeDtypeStruct((devices,) + block.shape, block.dtype),
        in_specs=[ANY],
        out_specs=ANY,
        scratch_shapes=[
            dma(()),
            dma((chips,)),
            dma((chips,)),
            dma((2 * chips,)),
            dma((chips + 1,)),
            dma((chips + 1,)),
            dma((2 * chips,)),
        ],
        compiler_params=params(collective),
        cost_estimate=pl.CostEstimate(
            flops=0, bytes_accessed=24 * devices * block.size, transcendentals=0
        ),
    )(block)
    return out.reshape(devices * block.shape[0], block.shape[1])


def reduce_kernel(
    chips, part, out, from_partner, summed, arrived, send_p, recv_p, send_z, recv_z
):
    me = lax.axis_index("seq")
    chip, core = me // 2, me % 2
    other = chip * 2 + 1 - core
    barrier = pltpu.get_barrier_semaphore()

    def greet(device):
        pl.semaphore_signal(barrier, inc=1, device_id={"seq": device}, device_id_type=MESH)

    greet(other)
    for t in range(1, chips):
        greet(((chip + t) % chips) * 2 + core)
    pl.semaphore_wait(barrier, chips)

    def to_partner(t):
        return pltpu.make_async_remote_copy(
            src_ref=part.at[((chip + t) % chips) * 2 + 1 - core],
            dst_ref=from_partner.at[t],
            send_sem=send_p.at[t],
            recv_sem=recv_p.at[t],
            device_id={"seq": other},
            device_id_type=MESH,
        )

    def to_owner(t):
        return pltpu.make_async_remote_copy(
            src_ref=summed.at[t],
            dst_ref=arrived.at[t],
            send_sem=send_z.at[t],
            recv_sem=recv_z.at[t],
            device_id={"seq": ((chip + t) % chips) * 2 + core},
            device_id_type=MESH,
        )

    order = list(range(1, chips)) + [0]
    for t in order:
        to_partner(t).start()
    for t in order:
        to_partner(t).wait()
        total = part[((chip + t) % chips) * 2 + core].astype(jnp.float32) + from_partner[t].astype(
            jnp.float32
        )
        if t:
            summed[t] = total.astype(summed.dtype)
            to_owner(t).start()
        else:
            out[...] = total
    for t in range(1, chips):
        to_owner(t).wait()
        out[...] += arrived[t].astype(jnp.float32)


def reduce_to_owner(part, devices, collective):
    chips = devices // 2
    rows, cols = part.shape[0] // devices, part.shape[1]
    dma = pltpu.SemaphoreType.DMA((chips,))
    slots = pltpu.VMEM((chips, rows, cols), part.dtype)
    return pl.pallas_call(
        functools.partial(reduce_kernel, chips),
        out_shape=jax.ShapeDtypeStruct((rows, cols), jnp.float32),
        in_specs=[VMEM],
        out_specs=VMEM,
        scratch_shapes=[slots, slots, slots, dma, dma, dma, dma],
        compiler_params=params(collective),
        cost_estimate=pl.CostEstimate(
            flops=0, bytes_accessed=24 * part.size, transcendentals=0
        ),
    )(part.reshape(devices, rows, cols))


def dot(left, right, contract):
    return lax.dot_general(
        left, right, ((contract[:1], contract[1:]), ((), ())), preferred_element_type=jnp.float32
    )


def attention_kernel(
    group, chunk, chips, pairs, mask, first, q, g, k, v, cos_t, sin_t, own, out, dkv, bias, scores,
    gprobs, weights, k_t, dk_sum, dv_sum, local_sem, send_r, send_l, send_p, recv_l, recv_r, recv_p
):
    step = pl.program_id(0)
    keys, tokens = bias.shape
    wide = 2 * HEAD
    me = lax.axis_index("seq")
    chip, core = me // 2, me % 2
    other = chip * 2 + 1 - core
    has_left, has_right = chip > 0, chip < chips - 1

    @pl.when(step == 0)
    def _():
        barrier = pltpu.get_barrier_semaphore()

        def greet(device):
            pl.semaphore_signal(barrier, inc=1, device_id={"seq": device}, device_id_type=MESH)

        greet(other)
        pl.when(has_left)(lambda: greet(me - 2))
        pl.when(has_right)(lambda: greet(me + 2))
        pl.semaphore_wait(barrier, 1 + has_left.astype(jnp.int32) + has_right.astype(jnp.int32))

    def columns_of(pair):
        start = pair * wide
        return pl.ds(start if isinstance(pair, int) else pl.multiple_of(start, wide), wide)

    def place(slot, pair):
        return out.at[slot, :, columns_of(pair)]

    def remote(pair, offset, send, recv, device):
        slot = me + 2 * offset
        return pltpu.make_async_remote_copy(
            src_ref=own.at[:, columns_of(pair)] if offset == 0 else place(slot, pair),
            dst_ref=place(slot, pair),
            send_sem=send,
            recv_sem=recv,
            device_id={"seq": device},
            device_id_type=MESH,
        )

    def right(pair, t):
        return remote(pair, -t, send_r.at[pair, t], recv_l.at[pair, t + 1], me + 2)

    def left(pair, t):
        return remote(pair, t, send_l.at[pair, t], recv_r.at[pair, t + 1], me - 2)

    def partner(pair, offset):
        at = offset + chips - 1
        return remote(pair, offset, send_p.at[pair, at], recv_p.at[pair, at], other)

    def arrival(slot, pair, sem):
        pltpu.make_async_copy(place(slot, pair), place(slot, pair), sem).wait()

    def stay(pair):
        return pltpu.make_async_copy(
            own.at[:, columns_of(pair)], place(me, pair), local_sem.at[pair]
        )

    def begin(pair):
        pl.when(has_right)(lambda: right(pair, 0).start())
        pl.when(has_left)(lambda: left(pair, 0).start())
        partner(pair, 0).start()
        stay(pair).start()

    def forward(pair, t):
        @pl.when(chip - t >= 0)
        def _():
            arrival(me - 2 * t, pair, recv_l.at[pair, t])
            if t < chips - 1:
                pl.when(has_right)(lambda: right(pair, t).start())
            partner(pair, -t).start()

        @pl.when(chip + t < chips)
        def _():
            arrival(me + 2 * t, pair, recv_r.at[pair, t])
            if t < chips - 1:
                pl.when(has_left)(lambda: left(pair, t).start())
            partner(pair, t).start()

    def finish(pair):
        stay(pair).wait()
        for t in range(chips):

            @pl.when(chip - t >= 0)
            def _():
                arrival(other - 2 * t, pair, recv_p.at[pair, chips - 1 - t])
                partner(pair, -t).wait_send()
                if t < chips - 1:
                    pl.when(has_right)(lambda: right(pair, t).wait_send())

            @pl.when(chip + t < chips)
            def _():
                if t > 0:
                    arrival(other + 2 * t, pair, recv_p.at[pair, chips - 1 + t])
                    partner(pair, t).wait_send()
                if t < chips - 1:
                    pl.when(has_left)(lambda: left(pair, t).wait_send())

    chunks = [pl.ds(c * chunk, chunk) for c in range(keys // chunk)]

    @pl.when(step == 0)
    def _():
        key_at = lax.broadcasted_iota(jnp.int32, (BLOCK, BLOCK), 0)
        query_at = lax.broadcasted_iota(jnp.int32, (BLOCK, BLOCK), 1)
        lower = jnp.where(key_at <= query_at, 0.0, -1e30).astype(jnp.float32)
        for i in range(tokens // BLOCK):
            def fill(j, _, i=i):
                shown = jnp.where(mask[i, j] == 1, 0.0, -1e30).astype(jnp.float32)
                inner = jnp.where(j == first[0] + i, 1.0, 0.0).astype(jnp.float32)
                rows = pl.ds(pl.multiple_of(j * BLOCK, BLOCK), BLOCK)
                bias[rows, i * BLOCK : (i + 1) * BLOCK] = lower * inner + shown
                return 0

            lax.fori_loop(0, keys // BLOCK, fill, 0)

    @pl.when(step % group == 0)
    def _():
        k_t[...] = k[...].T
        dk_sum[...] = jnp.zeros_like(dk_sum)
        dv_sum[...] = jnp.zeros_like(dv_sum)

    qh, gh = q[...], g[...]
    top = jnp.full((1, tokens), -3e38, jnp.float32)
    for at in chunks:
        s = dot(k[at, :], qh, (1, 1)) * (SCALE * LOG2E) + bias[at, :]
        scores[at, :] = s
        gprobs[at, :] = dot(v[at, :], gh, (1, 1))
        top = jnp.maximum(top, jnp.max(s, axis=0, keepdims=True))
    total = jnp.zeros((1, tokens), jnp.float32)
    for at in chunks:
        e = jnp.exp2(scores[at, :] - top)
        scores[at, :] = e
        total = total + jnp.sum(e, axis=0, keepdims=True)
    inverse = 1.0 / total
    row_dots = jnp.zeros((1, tokens), jnp.float32)
    for at in chunks:
        w = (scores[at, :] * inverse).astype(jnp.bfloat16)
        weights[at, :] = w
        row_dots = row_dots + jnp.sum(
            w.astype(jnp.float32) * gprobs[at, :], axis=0, keepdims=True
        )
    inverse_scaled = inverse * SCALE
    dq_t = jnp.zeros((HEAD, tokens), jnp.float32)
    for at in chunks:
        ds = ((scores[at, :] * inverse_scaled) * (gprobs[at, :] - row_dots)).astype(jnp.bfloat16)
        dk_sum[at, :] += dot(ds, qh, (1, 0))
        dv_sum[at, :] += dot(weights[at, :], gh, (1, 0))
        dq_t = dq_t + dot(k_t[:, at], ds, (1, 0))
    low, high = dq_t[:HALF, :], dq_t[HALF:, :]
    c, s = cos_t[...], sin_t[...]
    turned = jnp.concatenate([low * c + high * s, high * c - low * s], axis=0)
    own[:, pl.ds(pl.multiple_of(step * HEAD, HEAD), HEAD)] = turned.T.astype(jnp.bfloat16)

    @pl.when(step % group == group - 1)
    def _():
        head = step // group
        dkv[:, pl.ds(pl.multiple_of(head * HEAD, HEAD), HEAD)] = dk_sum[...].astype(jnp.bfloat16)
        at = pl.multiple_of(dkv.shape[1] // 2 + head * HEAD, HEAD)
        dkv[:, pl.ds(at, HEAD)] = dv_sum[...].astype(jnp.bfloat16)

    @pl.when(step % 2 == 1)
    def _():
        pair = step // 2
        begin(pair)
        for t in range(1, min(chips, pairs)):
            pl.when(pair - t >= 0)(lambda: forward(pair - t, t))

    @pl.when(step == 2 * pairs - 1)
    def _():
        for at in range(pairs, pairs + chips - 1):
            for t in range(1, chips):
                if at - t < pairs and at - t >= 0:
                    forward(at - t, t)
        for pair in range(pairs):
            finish(pair)


def attention(queries, grad_attn, keys_values, mask, first, cos_t, sin_t, kv_local, devices):
    tokens = queries.shape[0]
    heads = queries.shape[1] // HEAD
    group = heads // kv_local
    keys = keys_values.shape[0]
    f32, bf16 = jnp.float32, jnp.bfloat16
    chips, pairs = devices // 2, heads // 2
    dma = pltpu.SemaphoreType.DMA
    one_head = pl.BlockSpec((tokens, HEAD), lambda h: (0, h))
    angle = pl.BlockSpec((HALF, tokens), lambda h: (0, 0))
    smem = pl.BlockSpec(memory_space=pltpu.SMEM)
    return pl.pallas_call(
        functools.partial(attention_kernel, group, 512, chips, pairs),
        grid=(heads,),
        out_shape=[
            jax.ShapeDtypeStruct((tokens, heads * HEAD), bf16),
            jax.ShapeDtypeStruct((devices, tokens, heads * HEAD), bf16),
            jax.ShapeDtypeStruct((keys, 2 * kv_local * HEAD), bf16),
        ],
        in_specs=[
            smem,
            smem,
            one_head,
            one_head,
            pl.BlockSpec((keys, HEAD), lambda h: (0, h // group)),
            pl.BlockSpec((keys, HEAD), lambda h: (0, kv_local + h // group)),
            angle,
            angle,
        ],
        out_specs=[
            pl.BlockSpec((tokens, heads * HEAD), lambda h: (0, 0)),
            ANY,
            pl.BlockSpec((keys, 2 * kv_local * HEAD), lambda h: (0, 0)),
        ],
        scratch_shapes=[
            pltpu.VMEM((keys, tokens), f32),
            pltpu.VMEM((keys, tokens), f32),
            pltpu.VMEM((keys, tokens), f32),
            pltpu.VMEM((keys, tokens), bf16),
            pltpu.VMEM((HEAD, keys), bf16),
            pltpu.VMEM((keys, HEAD), f32),
            pltpu.VMEM((keys, HEAD), f32),
            dma((pairs,)),
            dma((pairs, chips)),
            dma((pairs, chips)),
            dma((pairs, 2 * chips)),
            dma((pairs, chips + 1)),
            dma((pairs, chips + 1)),
            dma((pairs, 2 * chips)),
        ],
        compiler_params=params(4, ("arbitrary",)),
        cost_estimate=pl.CostEstimate(
            flops=10 * keys * tokens * heads * HEAD,
            bytes_accessed=8 * keys * HEAD * kv_local,
            transcendentals=heads * keys * tokens,
        ),
    )(mask, first, queries, grad_attn, keys_values, keys_values, cos_t, sin_t)


def rotate(values, cosine, sine):
    rows = values.shape[0]
    pieces = values.reshape(rows, -1, HEAD)
    low, high = pieces[:, :, :HALF], pieces[:, :, HALF:]
    c, s = cosine[:, None, :], sine[:, None, :]
    return jnp.concatenate([low * c - high * s, high * c + low * s], axis=2).reshape(rows, -1)


def body(devices, groups, normed, w_query, w_key, w_value, positions, block_mask, grad_attn):
    tokens, width = normed.shape
    kv_cols = w_key.shape[1]
    kv_local = kv_cols // HEAD
    q_cols = w_query.shape[1]
    me = lax.axis_index("seq")
    part = width // devices // groups
    at = lax.axis_index("kvh") * part
    pieces = [
        lax.dynamic_slice_in_dim(normed, d * groups * part + at, part, 1) for d in range(devices)
    ]
    columns = lax.all_to_all(
        jnp.concatenate(pieces, axis=0), "seq", split_axis=0, concat_axis=0, tiled=True
    )
    columns = lax.all_gather(columns, "kvh", axis=1, tiled=True)

    frequency = THETA ** (-(jnp.arange(HALF, dtype=jnp.float32) * (2.0 / HEAD)))
    angles = positions.astype(jnp.float32)[:, None] * frequency[None, :]
    cosine, sine = jnp.cos(angles), jnp.sin(angles)

    def project(weight):
        return jnp.dot(normed, weight, preferred_element_type=jnp.float32)

    keys = rotate(project(w_key), cosine, sine).astype(jnp.bfloat16)
    values = project(w_value).astype(jnp.bfloat16)
    queries = rotate(project(w_query), cosine, sine).astype(jnp.bfloat16)
    keys_values = gather(jnp.concatenate([keys, values], axis=1), devices, 1)
    first = (me * (tokens // BLOCK)).astype(jnp.int32).reshape(1)
    dq, dq_all, dkv_part = attention(
        queries, grad_attn, keys_values, block_mask, first, cosine.T, sine.T, kv_local, devices
    )
    dq_all = dq_all.reshape(devices * tokens, q_cols)
    kv_total = reduce_to_owner(dkv_part, devices, 2)
    dk = rotate(kv_total[:, :kv_cols], cosine, -sine).astype(jnp.bfloat16)
    dv = kv_total[:, kv_cols:].astype(jnp.bfloat16)

    partial = dot(dq, w_query, (1, 1)) + dot(dk, w_key, (1, 1)) + dot(dv, w_value, (1, 1))
    grad_normed = lax.psum_scatter(
        partial.astype(jnp.bfloat16), "kvh", scatter_dimension=1, tiled=True
    )
    dkv_all = gather(jnp.concatenate([dk, dv], axis=1), devices, 3)
    grad_wq = dot(columns, dq_all, (0, 0))
    grad_wk = dot(columns, dkv_all[:, :kv_cols], (0, 0))
    grad_wv = dot(columns, dkv_all[:, kv_cols:], (0, 0))
    return (grad_normed, grad_wq, grad_wk, grad_wv)


def solution(mesh):
    in_specs = (
        P("seq", None),
        P(None, "kvh"),
        P(None, "kvh"),
        P(None, "kvh"),
        P("seq"),
        P("seq", None),
        P("seq", "kvh"),
    )
    out_specs = (P("seq", "kvh"),) * 4
    return jax.shard_map(
        functools.partial(body, mesh.shape["seq"], mesh.shape["kvh"]),
        mesh=mesh,
        in_specs=in_specs,
        out_specs=out_specs,
        check_vma=False,
    )
```

```python
import functools
import math

import jax
import jax.numpy as jnp
from jax import lax
from jax.experimental import pallas as pl
from jax.experimental.pallas import tpu as pltpu
from jax.sharding import PartitionSpec as P

HEAD = 128
HALF = 64
BLOCK = 128
THETA = 500000.0
SCALE = HEAD**-0.5
LOG2E = math.log2(math.e)
MESH = pl.DeviceIdType.MESH
ANY = pl.BlockSpec(memory_space=pl.ANY)
VMEM = pl.BlockSpec(memory_space=pltpu.VMEM)


def params(collective=None, semantics=None):
    extra = {}
    if collective is not None:
        extra = dict(collective_id=collective, has_side_effects=True)
    if semantics is not None:
        extra["dimension_semantics"] = semantics
    return pltpu.CompilerParams(vmem_limit_bytes=56 * 1024 * 1024, **extra)


def gather_kernel(chips, own, out, local_sem, send_r, send_l, send_p, recv_l, recv_r, recv_p):
    me = lax.axis_index("seq")
    chip, core = me // 2, me % 2
    has_left, has_right = chip > 0, chip < chips - 1
    mine = pltpu.make_async_copy(own, out.at[me], local_sem)
    mine.start()
    barrier = pltpu.get_barrier_semaphore()

    def greet(device):
        pl.semaphore_signal(barrier, inc=1, device_id={"seq": device}, device_id_type=MESH)

    greet(chip * 2 + 1 - core)
    pl.when(has_left)(lambda: greet(me - 2))
    pl.when(has_right)(lambda: greet(me + 2))
    pl.semaphore_wait(barrier, 1 + has_left.astype(jnp.int32) + has_right.astype(jnp.int32))

    def remote(src, slot, send, recv, device):
        return pltpu.make_async_remote_copy(
            src_ref=src,
            dst_ref=out.at[slot],
            send_sem=send,
            recv_sem=recv,
            device_id={"seq": device},
            device_id_type=MESH,
        )

    def source(distance, slot):
        return own if distance == 0 else out.at[slot]

    def right(t):
        slot = me - 2 * t
        return remote(source(t, slot), slot, send_r.at[t], recv_l.at[t + 1], me + 2)

    def left(t):
        slot = me + 2 * t
        return remote(source(t, slot), slot, send_l.at[t], recv_r.at[t + 1], me - 2)

    def partner(offset):
        slot = me + 2 * offset
        at = offset + chips - 1
        return remote(
            source(abs(offset), slot), slot, send_p.at[at], recv_p.at[at], chip * 2 + 1 - core
        )

    def arrival(slot, sem):
        pltpu.make_async_copy(out.at[slot], out.at[slot], sem).wait()

    pl.when(has_right)(lambda: right(0).start())
    pl.when(has_left)(lambda: left(0).start())
    partner(0).start()
    for t in range(1, chips):

        @pl.when(chip - t >= 0)
        def _():
            arrival(me - 2 * t, recv_l.at[t])
            if t < chips - 1:
                pl.when(has_right)(lambda: right(t).start())
            partner(-t).start()

        @pl.when(chip + t < chips)
        def _():
            arrival(me + 2 * t, recv_r.at[t])
            if t < chips - 1:
                pl.when(has_left)(lambda: left(t).start())
            partner(t).start()

    mine.wait()
    other = chip * 2 + 1 - core
    for t in range(chips):

        @pl.when(chip - t >= 0)
        def _():
            arrival(other - 2 * t, recv_p.at[chips - 1 - t])
            partner(-t).wait_send()
            if t < chips - 1:
                pl.when(has_right)(lambda: right(t).wait_send())

        @pl.when(chip + t < chips)
        def _():
            if t > 0:
                arrival(other + 2 * t, recv_p.at[chips - 1 + t])
                partner(t).wait_send()
            if t < chips - 1:
                pl.when(has_left)(lambda: left(t).wait_send())


def gather(block, devices, collective):
    chips = devices // 2
    dma = pltpu.SemaphoreType.DMA
    out = pl.pallas_call(
        functools.partial(gather_kernel, chips),
        out_shape=jax.ShapeDtypeStruct((devices,) + block.shape, block.dtype),
        in_specs=[ANY],
        out_specs=ANY,
        scratch_shapes=[
            dma(()),
            dma((chips,)),
            dma((chips,)),
            dma((2 * chips,)),
            dma((chips + 1,)),
            dma((chips + 1,)),
            dma((2 * chips,)),
        ],
        compiler_params=params(collective),
        cost_estimate=pl.CostEstimate(
            flops=0, bytes_accessed=24 * devices * block.size, transcendentals=0
        ),
    )(block)
    return out.reshape(devices * block.shape[0], block.shape[1])


def reduce_kernel(
    chips, part, out, from_partner, summed, arrived, send_p, recv_p, send_z, recv_z
):
    me = lax.axis_index("seq")
    chip, core = me // 2, me % 2
    other = chip * 2 + 1 - core
    barrier = pltpu.get_barrier_semaphore()

    def greet(device):
        pl.semaphore_signal(barrier, inc=1, device_id={"seq": device}, device_id_type=MESH)

    greet(other)
    for t in range(1, chips):
        greet(((chip + t) % chips) * 2 + core)
    pl.semaphore_wait(barrier, chips)

    def to_partner(t):
        return pltpu.make_async_remote_copy(
            src_ref=part.at[((chip + t) % chips) * 2 + 1 - core],
            dst_ref=from_partner.at[t],
            send_sem=send_p.at[t],
            recv_sem=recv_p.at[t],
            device_id={"seq": other},
            device_id_type=MESH,
        )

    def to_owner(t):
        return pltpu.make_async_remote_copy(
            src_ref=summed.at[t],
            dst_ref=arrived.at[t],
            send_sem=send_z.at[t],
            recv_sem=recv_z.at[t],
            device_id={"seq": ((chip + t) % chips) * 2 + core},
            device_id_type=MESH,
        )

    order = list(range(1, chips)) + [0]
    for t in order:
        to_partner(t).start()
    for t in order:
        to_partner(t).wait()
        total = part[((chip + t) % chips) * 2 + core].astype(jnp.float32) + from_partner[t].astype(
            jnp.float32
        )
        if t:
            summed[t] = total.astype(summed.dtype)
            to_owner(t).start()
        else:
            out[...] = total
    for t in range(1, chips):
        to_owner(t).wait()
        out[...] += arrived[t].astype(jnp.float32)


def reduce_to_owner(part, devices, collective):
    chips = devices // 2
    rows, cols = part.shape[0] // devices, part.shape[1]
    dma = pltpu.SemaphoreType.DMA((chips,))
    slots = pltpu.VMEM((chips, rows, cols), part.dtype)
    return pl.pallas_call(
        functools.partial(reduce_kernel, chips),
        out_shape=jax.ShapeDtypeStruct((rows, cols), jnp.float32),
        in_specs=[VMEM],
        out_specs=VMEM,
        scratch_shapes=[slots, slots, slots, dma, dma, dma, dma],
        compiler_params=params(collective),
        cost_estimate=pl.CostEstimate(
            flops=0, bytes_accessed=24 * part.size, transcendentals=0
        ),
    )(part.reshape(devices, rows, cols))


def dot(left, right, contract):
    return lax.dot_general(
        left, right, ((contract[:1], contract[1:]), ((), ())), preferred_element_type=jnp.float32
    )


def attention_kernel(
    group, chunk, chips, pairs, mask, first, q, g, k, v, cos_t, sin_t, own, out, dkv, bias, scores,
    gprobs, weights, k_t, dk_sum, dv_sum, local_sem, send_r, send_l, send_p, recv_l, recv_r, recv_p
):
    step = pl.program_id(0)
    keys, tokens = bias.shape
    wide = 2 * HEAD
    me = lax.axis_index("seq")
    chip, core = me // 2, me % 2
    other = chip * 2 + 1 - core
    has_left, has_right = chip > 0, chip < chips - 1

    @pl.when(step == 0)
    def _():
        barrier = pltpu.get_barrier_semaphore()

        def greet(device):
            pl.semaphore_signal(barrier, inc=1, device_id={"seq": device}, device_id_type=MESH)

        greet(other)
        pl.when(has_left)(lambda: greet(me - 2))
        pl.when(has_right)(lambda: greet(me + 2))
        pl.semaphore_wait(barrier, 1 + has_left.astype(jnp.int32) + has_right.astype(jnp.int32))

    def columns_of(pair):
        start = pair * wide
        return pl.ds(start if isinstance(pair, int) else pl.multiple_of(start, wide), wide)

    def place(slot, pair):
        return out.at[slot, :, columns_of(pair)]

    def remote(pair, offset, send, recv, device):
        slot = me + 2 * offset
        return pltpu.make_async_remote_copy(
            src_ref=own.at[:, columns_of(pair)] if offset == 0 else place(slot, pair),
            dst_ref=place(slot, pair),
            send_sem=send,
            recv_sem=recv,
            device_id={"seq": device},
            device_id_type=MESH,
        )

    def right(pair, t):
        return remote(pair, -t, send_r.at[pair, t], recv_l.at[pair, t + 1], me + 2)

    def left(pair, t):
        return remote(pair, t, send_l.at[pair, t], recv_r.at[pair, t + 1], me - 2)

    def partner(pair, offset):
        at = offset + chips - 1
        return remote(pair, offset, send_p.at[pair, at], recv_p.at[pair, at], other)

    def arrival(slot, pair, sem):
        pltpu.make_async_copy(place(slot, pair), place(slot, pair), sem).wait()

    def stay(pair):
        return pltpu.make_async_copy(
            own.at[:, columns_of(pair)], place(me, pair), local_sem.at[pair]
        )

    def begin(pair):
        pl.when(has_right)(lambda: right(pair, 0).start())
        pl.when(has_left)(lambda: left(pair, 0).start())
        partner(pair, 0).start()
        stay(pair).start()

    def forward(pair, t):
        @pl.when(chip - t >= 0)
        def _():
            arrival(me - 2 * t, pair, recv_l.at[pair, t])
            if t < chips - 1:
                pl.when(has_right)(lambda: right(pair, t).start())
            partner(pair, -t).start()

        @pl.when(chip + t < chips)
        def _():
            arrival(me + 2 * t, pair, recv_r.at[pair, t])
            if t < chips - 1:
                pl.when(has_left)(lambda: left(pair, t).start())
            partner(pair, t).start()

    def finish(pair):
        stay(pair).wait()
        for t in range(chips):

            @pl.when(chip - t >= 0)
            def _():
                arrival(other - 2 * t, pair, recv_p.at[pair, chips - 1 - t])
                partner(pair, -t).wait_send()
                if t < chips - 1:
                    pl.when(has_right)(lambda: right(pair, t).wait_send())

            @pl.when(chip + t < chips)
            def _():
                if t > 0:
                    arrival(other + 2 * t, pair, recv_p.at[pair, chips - 1 + t])
                    partner(pair, t).wait_send()
                if t < chips - 1:
                    pl.when(has_left)(lambda: left(pair, t).wait_send())

    chunks = [pl.ds(c * chunk, chunk) for c in range(keys // chunk)]

    @pl.when(step == 0)
    def _():
        key_at = lax.broadcasted_iota(jnp.int32, (BLOCK, BLOCK), 0)
        query_at = lax.broadcasted_iota(jnp.int32, (BLOCK, BLOCK), 1)
        lower = jnp.where(key_at <= query_at, 0.0, -1e30).astype(jnp.float32)
        for i in range(tokens // BLOCK):
            def fill(j, _, i=i):
                shown = jnp.where(mask[i, j] == 1, 0.0, -1e30).astype(jnp.float32)
                inner = jnp.where(j == first[0] + i, 1.0, 0.0).astype(jnp.float32)
                rows = pl.ds(pl.multiple_of(j * BLOCK, BLOCK), BLOCK)
                bias[rows, i * BLOCK : (i + 1) * BLOCK] = lower * inner + shown
                return 0

            lax.fori_loop(0, keys // BLOCK, fill, 0)

    @pl.when(step % group == 0)
    def _():
        k_t[...] = k[...].T
        dk_sum[...] = jnp.zeros_like(dk_sum)
        dv_sum[...] = jnp.zeros_like(dv_sum)

    qh, gh = q[...], g[...]
    top = jnp.full((1, tokens), -3e38, jnp.float32)
    for at in chunks:
        s = dot(k[at, :], qh, (1, 1)) * (SCALE * LOG2E) + bias[at, :]
        scores[at, :] = s
        gprobs[at, :] = dot(v[at, :], gh, (1, 1))
        top = jnp.maximum(top, jnp.max(s, axis=0, keepdims=True))
    total = jnp.zeros((1, tokens), jnp.float32)
    for at in chunks:
        e = jnp.exp2(scores[at, :] - top)
        scores[at, :] = e
        total = total + jnp.sum(e, axis=0, keepdims=True)
    inverse = 1.0 / total
    row_dots = jnp.zeros((1, tokens), jnp.float32)
    for at in chunks:
        w = (scores[at, :] * inverse).astype(jnp.bfloat16)
        weights[at, :] = w
        row_dots = row_dots + jnp.sum(
            w.astype(jnp.float32) * gprobs[at, :], axis=0, keepdims=True
        )
    inverse_scaled = inverse * SCALE
    dq_t = jnp.zeros((HEAD, tokens), jnp.float32)
    for at in chunks:
        ds = ((scores[at, :] * inverse_scaled) * (gprobs[at, :] - row_dots)).astype(jnp.bfloat16)
        dk_sum[at, :] += dot(ds, qh, (1, 0))
        dv_sum[at, :] += dot(weights[at, :], gh, (1, 0))
        dq_t = dq_t + dot(k_t[:, at], ds, (1, 0))
    low, high = dq_t[:HALF, :], dq_t[HALF:, :]
    c, s = cos_t[...], sin_t[...]
    turned = jnp.concatenate([low * c + high * s, high * c - low * s], axis=0)
    own[:, pl.ds(pl.multiple_of(step * HEAD, HEAD), HEAD)] = turned.T.astype(jnp.bfloat16)

    @pl.when(step % group == group - 1)
    def _():
        head = step // group
        dkv[:, pl.ds(pl.multiple_of(head * HEAD, HEAD), HEAD)] = dk_sum[...].astype(jnp.bfloat16)
        at = pl.multiple_of(dkv.shape[1] // 2 + head * HEAD, HEAD)
        dkv[:, pl.ds(at, HEAD)] = dv_sum[...].astype(jnp.bfloat16)

    @pl.when(step % 2 == 1)
    def _():
        pair = step // 2
        begin(pair)
        for t in range(1, min(chips, pairs)):
            pl.when(pair - t >= 0)(lambda: forward(pair - t, t))

    @pl.when(step == 2 * pairs - 1)
    def _():
        for at in range(pairs, pairs + chips - 1):
            for t in range(1, chips):
                if at - t < pairs and at - t >= 0:
                    forward(at - t, t)
        for pair in range(pairs):
            finish(pair)


def attention(queries, grad_attn, keys_values, mask, first, cos_t, sin_t, kv_local, devices):
    tokens = queries.shape[0]
    heads = queries.shape[1] // HEAD
    group = heads // kv_local
    keys = keys_values.shape[0]
    f32, bf16 = jnp.float32, jnp.bfloat16
    chips, pairs = devices // 2, heads // 2
    dma = pltpu.SemaphoreType.DMA
    one_head = pl.BlockSpec((tokens, HEAD), lambda h: (0, h))
    angle = pl.BlockSpec((HALF, tokens), lambda h: (0, 0))
    smem = pl.BlockSpec(memory_space=pltpu.SMEM)
    return pl.pallas_call(
        functools.partial(attention_kernel, group, 512, chips, pairs),
        grid=(heads,),
        out_shape=[
            jax.ShapeDtypeStruct((tokens, heads * HEAD), bf16),
            jax.ShapeDtypeStruct((devices, tokens, heads * HEAD), bf16),
            jax.ShapeDtypeStruct((keys, 2 * kv_local * HEAD), bf16),
        ],
        in_specs=[
            smem,
            smem,
            one_head,
            one_head,
            pl.BlockSpec((keys, HEAD), lambda h: (0, h // group)),
            pl.BlockSpec((keys, HEAD), lambda h: (0, kv_local + h // group)),
            angle,
            angle,
        ],
        out_specs=[
            pl.BlockSpec((tokens, heads * HEAD), lambda h: (0, 0)),
            ANY,
            pl.BlockSpec((keys, 2 * kv_local * HEAD), lambda h: (0, 0)),
        ],
        scratch_shapes=[
            pltpu.VMEM((keys, tokens), f32),
            pltpu.VMEM((keys, tokens), f32),
            pltpu.VMEM((keys, tokens), f32),
            pltpu.VMEM((keys, tokens), bf16),
            pltpu.VMEM((HEAD, keys), bf16),
            pltpu.VMEM((keys, HEAD), f32),
            pltpu.VMEM((keys, HEAD), f32),
            dma((pairs,)),
            dma((pairs, chips)),
            dma((pairs, chips)),
            dma((pairs, 2 * chips)),
            dma((pairs, chips + 1)),
            dma((pairs, chips + 1)),
            dma((pairs, 2 * chips)),
        ],
        compiler_params=params(4, ("arbitrary",)),
        cost_estimate=pl.CostEstimate(
            flops=10 * keys * tokens * heads * HEAD,
            bytes_accessed=8 * keys * HEAD * kv_local,
            transcendentals=heads * keys * tokens,
        ),
    )(mask, first, queries, grad_attn, keys_values, keys_values, cos_t, sin_t)


def rotate(values, cosine, sine):
    rows = values.shape[0]
    pieces = values.reshape(rows, -1, HEAD)
    low, high = pieces[:, :, :HALF], pieces[:, :, HALF:]
    c, s = cosine[:, None, :], sine[:, None, :]
    return jnp.concatenate([low * c - high * s, high * c + low * s], axis=2).reshape(rows, -1)


def body(devices, groups, normed, w_query, w_key, w_value, positions, block_mask, grad_attn):
    tokens, width = normed.shape
    kv_cols = w_key.shape[1]
    kv_local = kv_cols // HEAD
    q_cols = w_query.shape[1]
    me = lax.axis_index("seq")
    part = width // devices // groups
    my_part = lax.dynamic_slice_in_dim(
        normed.reshape(tokens, devices, groups * part), lax.axis_index("kvh") * part, part, 2
    )
    columns = lax.all_to_all(
        my_part.reshape(tokens, devices * part), "seq", split_axis=1, concat_axis=0, tiled=True
    )
    columns = lax.all_gather(columns, "kvh", axis=1, tiled=True)

    frequency = THETA ** (-(jnp.arange(HALF, dtype=jnp.float32) * (2.0 / HEAD)))
    angles = positions.astype(jnp.float32)[:, None] * frequency[None, :]
    cosine, sine = jnp.cos(angles), jnp.sin(angles)

    def project(weight):
        return jnp.dot(normed, weight, preferred_element_type=jnp.float32)

    keys = rotate(project(w_key), cosine, sine).astype(jnp.bfloat16)
    values = project(w_value).astype(jnp.bfloat16)
    queries = rotate(project(w_query), cosine, sine).astype(jnp.bfloat16)
    keys_values = gather(jnp.concatenate([keys, values], axis=1), devices, 1)
    first = (me * (tokens // BLOCK)).astype(jnp.int32).reshape(1)
    dq, dq_all, dkv_part = attention(
        queries, grad_attn, keys_values, block_mask, first, cosine.T, sine.T, kv_local, devices
    )
    dq_all = dq_all.reshape(devices * tokens, q_cols)
    kv_total = reduce_to_owner(dkv_part, devices, 2)
    dk = rotate(kv_total[:, :kv_cols], cosine, -sine).astype(jnp.bfloat16)
    dv = kv_total[:, kv_cols:].astype(jnp.bfloat16)

    partial = dot(dq, w_query, (1, 1)) + dot(dk, w_key, (1, 1)) + dot(dv, w_value, (1, 1))
    grad_normed = lax.psum_scatter(
        partial.astype(jnp.bfloat16), "kvh", scatter_dimension=1, tiled=True
    )
    dkv_all = gather(jnp.concatenate([dk, dv], axis=1), devices, 3)
    grad_wq = dot(columns, dq_all, (0, 0))
    grad_wk = dot(columns, dkv_all[:, :kv_cols], (0, 0))
    grad_wv = dot(columns, dkv_all[:, kv_cols:], (0, 0))
    return (grad_normed, grad_wq, grad_wk, grad_wv)


def solution(mesh):
    in_specs = (
        P("seq", None),
        P(None, "kvh"),
        P(None, "kvh"),
        P(None, "kvh"),
        P("seq"),
        P("seq", None),
        P("seq", "kvh"),
    )
    out_specs = (P("seq", "kvh"),) * 4
    return jax.shard_map(
        functools.partial(body, mesh.shape["seq"], mesh.shape["kvh"]),
        mesh=mesh,
        in_specs=in_specs,
        out_specs=out_specs,
        check_vma=False,
    )
```

```python
import functools
import math

import jax
import jax.numpy as jnp
from jax import lax
from jax.experimental import pallas as pl
from jax.experimental.pallas import tpu as pltpu
from jax.sharding import PartitionSpec as P

HEAD = 128
HALF = 64
BLOCK = 128
THETA = 500000.0
SCALE = HEAD**-0.5
LOG2E = math.log2(math.e)
MESH = pl.DeviceIdType.MESH
ANY = pl.BlockSpec(memory_space=pl.ANY)
VMEM = pl.BlockSpec(memory_space=pltpu.VMEM)


def params(collective=None, semantics=None):
    extra = {}
    if collective is not None:
        extra = dict(collective_id=collective, has_side_effects=True)
    if semantics is not None:
        extra["dimension_semantics"] = semantics
    return pltpu.CompilerParams(vmem_limit_bytes=56 * 1024 * 1024, **extra)


def gather_kernel(chips, own, out, local_sem, send_r, send_l, send_p, recv_l, recv_r, recv_p):
    me = lax.axis_index("seq")
    chip, core = me // 2, me % 2
    has_left, has_right = chip > 0, chip < chips - 1
    mine = pltpu.make_async_copy(own, out.at[me], local_sem)
    mine.start()
    barrier = pltpu.get_barrier_semaphore()

    def greet(device):
        pl.semaphore_signal(barrier, inc=1, device_id={"seq": device}, device_id_type=MESH)

    greet(chip * 2 + 1 - core)
    pl.when(has_left)(lambda: greet(me - 2))
    pl.when(has_right)(lambda: greet(me + 2))
    pl.semaphore_wait(barrier, 1 + has_left.astype(jnp.int32) + has_right.astype(jnp.int32))

    def remote(src, slot, send, recv, device):
        return pltpu.make_async_remote_copy(
            src_ref=src,
            dst_ref=out.at[slot],
            send_sem=send,
            recv_sem=recv,
            device_id={"seq": device},
            device_id_type=MESH,
        )

    def source(distance, slot):
        return own if distance == 0 else out.at[slot]

    def right(t):
        slot = me - 2 * t
        return remote(source(t, slot), slot, send_r.at[t], recv_l.at[t + 1], me + 2)

    def left(t):
        slot = me + 2 * t
        return remote(source(t, slot), slot, send_l.at[t], recv_r.at[t + 1], me - 2)

    def partner(offset):
        slot = me + 2 * offset
        at = offset + chips - 1
        return remote(
            source(abs(offset), slot), slot, send_p.at[at], recv_p.at[at], chip * 2 + 1 - core
        )

    def arrival(slot, sem):
        pltpu.make_async_copy(out.at[slot], out.at[slot], sem).wait()

    pl.when(has_right)(lambda: right(0).start())
    pl.when(has_left)(lambda: left(0).start())
    partner(0).start()
    for t in range(1, chips):

        @pl.when(chip - t >= 0)
        def _():
            arrival(me - 2 * t, recv_l.at[t])
            if t < chips - 1:
                pl.when(has_right)(lambda: right(t).start())
            partner(-t).start()

        @pl.when(chip + t < chips)
        def _():
            arrival(me + 2 * t, recv_r.at[t])
            if t < chips - 1:
                pl.when(has_left)(lambda: left(t).start())
            partner(t).start()

    mine.wait()
    other = chip * 2 + 1 - core
    for t in range(chips):

        @pl.when(chip - t >= 0)
        def _():
            arrival(other - 2 * t, recv_p.at[chips - 1 - t])
            partner(-t).wait_send()
            if t < chips - 1:
                pl.when(has_right)(lambda: right(t).wait_send())

        @pl.when(chip + t < chips)
        def _():
            if t > 0:
                arrival(other + 2 * t, recv_p.at[chips - 1 + t])
                partner(t).wait_send()
            if t < chips - 1:
                pl.when(has_left)(lambda: left(t).wait_send())


def gather(block, devices, collective):
    chips = devices // 2
    dma = pltpu.SemaphoreType.DMA
    out = pl.pallas_call(
        functools.partial(gather_kernel, chips),
        out_shape=jax.ShapeDtypeStruct((devices,) + block.shape, block.dtype),
        in_specs=[ANY],
        out_specs=ANY,
        scratch_shapes=[
            dma(()),
            dma((chips,)),
            dma((chips,)),
            dma((2 * chips,)),
            dma((chips + 1,)),
            dma((chips + 1,)),
            dma((2 * chips,)),
        ],
        compiler_params=params(collective),
        cost_estimate=pl.CostEstimate(
            flops=0, bytes_accessed=24 * devices * block.size, transcendentals=0
        ),
    )(block)
    return out.reshape(devices * block.shape[0], block.shape[1])


def reduce_kernel(
    chips, part, out, from_partner, summed, arrived, send_p, recv_p, send_z, recv_z
):
    me = lax.axis_index("seq")
    chip, core = me // 2, me % 2
    other = chip * 2 + 1 - core
    barrier = pltpu.get_barrier_semaphore()

    def greet(device):
        pl.semaphore_signal(barrier, inc=1, device_id={"seq": device}, device_id_type=MESH)

    greet(other)
    for t in range(1, chips):
        greet(((chip + t) % chips) * 2 + core)
    pl.semaphore_wait(barrier, chips)

    def to_partner(t):
        return pltpu.make_async_remote_copy(
            src_ref=part.at[((chip + t) % chips) * 2 + 1 - core],
            dst_ref=from_partner.at[t],
            send_sem=send_p.at[t],
            recv_sem=recv_p.at[t],
            device_id={"seq": other},
            device_id_type=MESH,
        )

    def to_owner(t):
        return pltpu.make_async_remote_copy(
            src_ref=summed.at[t],
            dst_ref=arrived.at[t],
            send_sem=send_z.at[t],
            recv_sem=recv_z.at[t],
            device_id={"seq": ((chip + t) % chips) * 2 + core},
            device_id_type=MESH,
        )

    order = list(range(1, chips)) + [0]
    for t in order:
        to_partner(t).start()
    for t in order:
        to_partner(t).wait()
        total = part[((chip + t) % chips) * 2 + core].astype(jnp.float32) + from_partner[t].astype(
            jnp.float32
        )
        if t:
            summed[t] = total.astype(summed.dtype)
            to_owner(t).start()
        else:
            out[...] = total
    for t in range(1, chips):
        to_owner(t).wait()
        out[...] += arrived[t].astype(jnp.float32)


def reduce_to_owner(part, devices, collective):
    chips = devices // 2
    rows, cols = part.shape[0] // devices, part.shape[1]
    dma = pltpu.SemaphoreType.DMA((chips,))
    slots = pltpu.VMEM((chips, rows, cols), part.dtype)
    return pl.pallas_call(
        functools.partial(reduce_kernel, chips),
        out_shape=jax.ShapeDtypeStruct((rows, cols), jnp.float32),
        in_specs=[VMEM],
        out_specs=VMEM,
        scratch_shapes=[slots, slots, slots, dma, dma, dma, dma],
        compiler_params=params(collective),
        cost_estimate=pl.CostEstimate(
            flops=0, bytes_accessed=24 * part.size, transcendentals=0
        ),
    )(part.reshape(devices, rows, cols))


def dot(left, right, contract):
    return lax.dot_general(
        left, right, ((contract[:1], contract[1:]), ((), ())), preferred_element_type=jnp.float32
    )


def attention_kernel(
    group, chunk, chips, pairs, mask, first, q, g, k, v, cos_t, sin_t, own, out, dkv, bias, scores,
    gprobs, weights, k_t, dk_sum, dv_sum, local_sem, send_r, send_l, send_p, recv_l, recv_r, recv_p
):
    step = pl.program_id(0)
    keys, tokens = bias.shape
    wide = 2 * HEAD
    me = lax.axis_index("seq")
    chip, core = me // 2, me % 2
    other = chip * 2 + 1 - core
    has_left, has_right = chip > 0, chip < chips - 1

    @pl.when(step == 0)
    def _():
        barrier = pltpu.get_barrier_semaphore()

        def greet(device):
            pl.semaphore_signal(barrier, inc=1, device_id={"seq": device}, device_id_type=MESH)

        greet(other)
        pl.when(has_left)(lambda: greet(me - 2))
        pl.when(has_right)(lambda: greet(me + 2))
        pl.semaphore_wait(barrier, 1 + has_left.astype(jnp.int32) + has_right.astype(jnp.int32))

    def columns_of(pair):
        start = pair * wide
        return pl.ds(start if isinstance(pair, int) else pl.multiple_of(start, wide), wide)

    def place(slot, pair):
        return out.at[slot, :, columns_of(pair)]

    def remote(pair, offset, send, recv, device):
        slot = me + 2 * offset
        return pltpu.make_async_remote_copy(
            src_ref=own.at[:, columns_of(pair)] if offset == 0 else place(slot, pair),
            dst_ref=place(slot, pair),
            send_sem=send,
            recv_sem=recv,
            device_id={"seq": device},
            device_id_type=MESH,
        )

    def right(pair, t):
        return remote(pair, -t, send_r.at[pair, t], recv_l.at[pair, t + 1], me + 2)

    def left(pair, t):
        return remote(pair, t, send_l.at[pair, t], recv_r.at[pair, t + 1], me - 2)

    def partner(pair, offset):
        at = offset + chips - 1
        return remote(pair, offset, send_p.at[pair, at], recv_p.at[pair, at], other)

    def arrival(slot, pair, sem):
        pltpu.make_async_copy(place(slot, pair), place(slot, pair), sem).wait()

    def stay(pair):
        return pltpu.make_async_copy(
            own.at[:, columns_of(pair)], place(me, pair), local_sem.at[pair]
        )

    def begin(pair):
        pl.when(has_right)(lambda: right(pair, 0).start())
        pl.when(has_left)(lambda: left(pair, 0).start())
        partner(pair, 0).start()
        stay(pair).start()

    def forward(pair, t):
        @pl.when(chip - t >= 0)
        def _():
            arrival(me - 2 * t, pair, recv_l.at[pair, t])
            if t < chips - 1:
                pl.when(has_right)(lambda: right(pair, t).start())
            partner(pair, -t).start()

        @pl.when(chip + t < chips)
        def _():
            arrival(me + 2 * t, pair, recv_r.at[pair, t])
            if t < chips - 1:
                pl.when(has_left)(lambda: left(pair, t).start())
            partner(pair, t).start()

    def finish(pair):
        stay(pair).wait()
        for t in range(chips):

            @pl.when(chip - t >= 0)
            def _():
                arrival(other - 2 * t, pair, recv_p.at[pair, chips - 1 - t])
                partner(pair, -t).wait_send()
                if t < chips - 1:
                    pl.when(has_right)(lambda: right(pair, t).wait_send())

            @pl.when(chip + t < chips)
            def _():
                if t > 0:
                    arrival(other + 2 * t, pair, recv_p.at[pair, chips - 1 + t])
                    partner(pair, t).wait_send()
                if t < chips - 1:
                    pl.when(has_left)(lambda: left(pair, t).wait_send())

    chunks = [pl.ds(c * chunk, chunk) for c in range(keys // chunk)]

    @pl.when(step == 0)
    def _():
        key_at = lax.broadcasted_iota(jnp.int32, (BLOCK, BLOCK), 0)
        query_at = lax.broadcasted_iota(jnp.int32, (BLOCK, BLOCK), 1)
        lower = jnp.where(key_at <= query_at, 0.0, -1e30).astype(jnp.float32)
        for i in range(tokens // BLOCK):
            def fill(j, _, i=i):
                shown = jnp.where(mask[i, j] == 1, 0.0, -1e30).astype(jnp.float32)
                inner = jnp.where(j == first[0] + i, 1.0, 0.0).astype(jnp.float32)
                rows = pl.ds(pl.multiple_of(j * BLOCK, BLOCK), BLOCK)
                bias[rows, i * BLOCK : (i + 1) * BLOCK] = lower * inner + shown
                return 0

            lax.fori_loop(0, keys // BLOCK, fill, 0)

    @pl.when(step % group == 0)
    def _():
        k_t[...] = k[...].T
        dk_sum[...] = jnp.zeros_like(dk_sum)
        dv_sum[...] = jnp.zeros_like(dv_sum)

    qh, gh = q[...], g[...]
    top = jnp.full((1, tokens), -3e38, jnp.float32)
    for at in chunks:
        s = dot(k[at, :], qh, (1, 1)) * (SCALE * LOG2E) + bias[at, :]
        scores[at, :] = s
        gprobs[at, :] = dot(v[at, :], gh, (1, 1))
        top = jnp.maximum(top, jnp.max(s, axis=0, keepdims=True))
    total = jnp.zeros((1, tokens), jnp.float32)
    for at in chunks:
        e = jnp.exp2(scores[at, :] - top)
        scores[at, :] = e
        total = total + jnp.sum(e, axis=0, keepdims=True)
    inverse = 1.0 / total
    row_dots = jnp.zeros((1, tokens), jnp.float32)
    for at in chunks:
        w = (scores[at, :] * inverse).astype(jnp.bfloat16)
        weights[at, :] = w
        row_dots = row_dots + jnp.sum(
            w.astype(jnp.float32) * gprobs[at, :], axis=0, keepdims=True
        )
    inverse_scaled = inverse * SCALE
    dq_t = jnp.zeros((HEAD, tokens), jnp.float32)
    for at in chunks:
        ds = ((scores[at, :] * inverse_scaled) * (gprobs[at, :] - row_dots)).astype(jnp.bfloat16)
        dk_sum[at, :] += dot(ds, qh, (1, 0))
        dv_sum[at, :] += dot(weights[at, :], gh, (1, 0))
        dq_t = dq_t + dot(k_t[:, at], ds, (1, 0))
    low, high = dq_t[:HALF, :], dq_t[HALF:, :]
    c, s = cos_t[...], sin_t[...]
    turned = jnp.concatenate([low * c + high * s, high * c - low * s], axis=0)
    own[:, pl.ds(pl.multiple_of(step * HEAD, HEAD), HEAD)] = turned.T.astype(jnp.bfloat16)

    @pl.when(step % group == group - 1)
    def _():
        head = step // group
        dkv[:, pl.ds(pl.multiple_of(head * HEAD, HEAD), HEAD)] = dk_sum[...].astype(jnp.bfloat16)
        at = pl.multiple_of(dkv.shape[1] // 2 + head * HEAD, HEAD)
        dkv[:, pl.ds(at, HEAD)] = dv_sum[...].astype(jnp.bfloat16)

    @pl.when(step % 2 == 1)
    def _():
        pair = step // 2
        begin(pair)
        for t in range(1, min(chips, pairs)):
            pl.when(pair - t >= 0)(lambda: forward(pair - t, t))

    @pl.when(step == 2 * pairs - 1)
    def _():
        for at in range(pairs, pairs + chips - 1):
            for t in range(1, chips):
                if at - t < pairs and at - t >= 0:
                    forward(at - t, t)
        for pair in range(pairs):
            finish(pair)


def attention(queries, grad_attn, keys_values, mask, first, cos_t, sin_t, kv_local, devices):
    tokens = queries.shape[0]
    heads = queries.shape[1] // HEAD
    group = heads // kv_local
    keys = keys_values.shape[0]
    f32, bf16 = jnp.float32, jnp.bfloat16
    chips, pairs = devices // 2, heads // 2
    dma = pltpu.SemaphoreType.DMA
    one_head = pl.BlockSpec((tokens, HEAD), lambda h: (0, h))
    angle = pl.BlockSpec((HALF, tokens), lambda h: (0, 0))
    smem = pl.BlockSpec(memory_space=pltpu.SMEM)
    return pl.pallas_call(
        functools.partial(attention_kernel, group, 512, chips, pairs),
        grid=(heads,),
        out_shape=[
            jax.ShapeDtypeStruct((tokens, heads * HEAD), bf16),
            jax.ShapeDtypeStruct((devices, tokens, heads * HEAD), bf16),
            jax.ShapeDtypeStruct((keys, 2 * kv_local * HEAD), bf16),
        ],
        in_specs=[
            smem,
            smem,
            one_head,
            one_head,
            pl.BlockSpec((keys, HEAD), lambda h: (0, h // group)),
            pl.BlockSpec((keys, HEAD), lambda h: (0, kv_local + h // group)),
            angle,
            angle,
        ],
        out_specs=[
            pl.BlockSpec((tokens, heads * HEAD), lambda h: (0, 0)),
            ANY,
            pl.BlockSpec((keys, 2 * kv_local * HEAD), lambda h: (0, 0)),
        ],
        scratch_shapes=[
            pltpu.VMEM((keys, tokens), f32),
            pltpu.VMEM((keys, tokens), f32),
            pltpu.VMEM((keys, tokens), f32),
            pltpu.VMEM((keys, tokens), bf16),
            pltpu.VMEM((HEAD, keys), bf16),
            pltpu.VMEM((keys, HEAD), f32),
            pltpu.VMEM((keys, HEAD), f32),
            dma((pairs,)),
            dma((pairs, chips)),
            dma((pairs, chips)),
            dma((pairs, 2 * chips)),
            dma((pairs, chips + 1)),
            dma((pairs, chips + 1)),
            dma((pairs, 2 * chips)),
        ],
        compiler_params=params(4, ("arbitrary",)),
        cost_estimate=pl.CostEstimate(
            flops=10 * keys * tokens * heads * HEAD,
            bytes_accessed=8 * keys * HEAD * kv_local,
            transcendentals=heads * keys * tokens,
        ),
    )(mask, first, queries, grad_attn, keys_values, keys_values, cos_t, sin_t)


def take_kernel(index, source, out):
    out[...] = source[...]


def take_columns(normed, index, devices, groups, part):
    tokens = normed.shape[0]
    return pl.pallas_call(
        take_kernel,
        out_shape=jax.ShapeDtypeStruct((devices * tokens, part), normed.dtype),
        grid_spec=pltpu.PrefetchScalarGridSpec(
            num_scalar_prefetch=1,
            grid=(devices,),
            in_specs=[pl.BlockSpec((tokens, part), lambda d, at: (0, d * groups + at[0]))],
            out_specs=pl.BlockSpec((tokens, part), lambda d, at: (d, 0)),
        ),
    )(index.astype(jnp.int32).reshape(1), normed)


def rotate(values, cosine, sine):
    rows = values.shape[0]
    pieces = values.reshape(rows, -1, HEAD)
    low, high = pieces[:, :, :HALF], pieces[:, :, HALF:]
    c, s = cosine[:, None, :], sine[:, None, :]
    return jnp.concatenate([low * c - high * s, high * c + low * s], axis=2).reshape(rows, -1)


def body(devices, groups, normed, w_query, w_key, w_value, positions, block_mask, grad_attn):
    tokens, width = normed.shape
    kv_cols = w_key.shape[1]
    kv_local = kv_cols // HEAD
    q_cols = w_query.shape[1]
    me = lax.axis_index("seq")
    part = width // devices // groups
    index = lax.axis_index("kvh")
    if part % HEAD == 0:
        pieces = take_columns(normed, index, devices, groups, part)
    else:
        wide = normed.reshape(tokens, devices, groups * part)
        pieces = lax.dynamic_slice_in_dim(wide, index * part, part, 2)
        pieces = jnp.transpose(pieces, (1, 0, 2)).reshape(devices * tokens, part)
    columns = lax.all_to_all(pieces, "seq", split_axis=0, concat_axis=0, tiled=True)
    columns = lax.all_gather(columns, "kvh", axis=1, tiled=True)

    frequency = THETA ** (-(jnp.arange(HALF, dtype=jnp.float32) * (2.0 / HEAD)))
    angles = positions.astype(jnp.float32)[:, None] * frequency[None, :]
    cosine, sine = jnp.cos(angles), jnp.sin(angles)

    def project(weight):
        return jnp.dot(normed, weight, preferred_element_type=jnp.float32)

    keys = rotate(project(w_key), cosine, sine).astype(jnp.bfloat16)
    values = project(w_value).astype(jnp.bfloat16)
    queries = rotate(project(w_query), cosine, sine).astype(jnp.bfloat16)
    keys_values = gather(jnp.concatenate([keys, values], axis=1), devices, 1)
    first = (me * (tokens // BLOCK)).astype(jnp.int32).reshape(1)
    dq, dq_all, dkv_part = attention(
        queries, grad_attn, keys_values, block_mask, first, cosine.T, sine.T, kv_local, devices
    )
    dq_all = dq_all.reshape(devices * tokens, q_cols)
    kv_total = reduce_to_owner(dkv_part, devices, 2)
    dk = rotate(kv_total[:, :kv_cols], cosine, -sine).astype(jnp.bfloat16)
    dv = kv_total[:, kv_cols:].astype(jnp.bfloat16)

    partial = dot(dq, w_query, (1, 1)) + dot(dk, w_key, (1, 1)) + dot(dv, w_value, (1, 1))
    grad_normed = lax.psum_scatter(
        partial.astype(jnp.bfloat16), "kvh", scatter_dimension=1, tiled=True
    )
    dkv_all = gather(jnp.concatenate([dk, dv], axis=1), devices, 3)
    grad_wq = dot(columns, dq_all, (0, 0))
    grad_wk = dot(columns, dkv_all[:, :kv_cols], (0, 0))
    grad_wv = dot(columns, dkv_all[:, kv_cols:], (0, 0))
    return (grad_normed, grad_wq, grad_wk, grad_wv)


def solution(mesh):
    in_specs = (
        P("seq", None),
        P(None, "kvh"),
        P(None, "kvh"),
        P(None, "kvh"),
        P("seq"),
        P("seq", None),
        P("seq", "kvh"),
    )
    out_specs = (P("seq", "kvh"),) * 4
    return jax.shard_map(
        functools.partial(body, mesh.shape["seq"], mesh.shape["kvh"]),
        mesh=mesh,
        in_specs=in_specs,
        out_specs=out_specs,
        check_vma=False,
    )
```
